32 devices in a mesh: frag: 2 (over x), pair: 16 (over z, y, core).
Axes of the slice: x: 2, y: 2, z: 4, core: 2. Of those that a mesh axis runs over, the one named last changes fastest.
Arguments:
- amplitudes: bfloat16 [64, 640, 640], P(('frag', 'pair')), parts along dimension 0, may hold values from -6 to 6
- pair_ints: bfloat16 [64, 640, 640], P(('frag', 'pair')), parts along dimension 0, may hold values from -6 to 6
- int_tiles: bfloat16 [128, 128, 128], P(('frag', 'pair')), parts along dimension 0, may hold values from -0.25 to 0.25
- tile_owner: int32 [4000, 1], P('frag'), parts along dimension 0, may hold values from 0 to 15; in each aligned block of 125 rows (0 to 124, 125 to 249, ...) at most 16 rows name the same one
- tile_slot: int32 [4000], P('frag'), parts along dimension 0, may hold values from 0 to 3
- tile_extent: int32 [32, 5], P(('frag', 'pair')), parts along dimension 0, may hold values from 64 to 128, as said below
- tile_mask: int32 [64, 5, 5], P(('frag', 'pair')), parts along dimension 0, may hold values 0 or 1
- mirror_slot: int32 [64], P(('frag', 'pair')), parts along dimension 0, may hold values from 0 to 1, as said below
Outputs:
- residual: float32 [64, 640, 640], P(('frag', 'pair')), parts along dimension 0
The draws below stay inside these ranges and needn't reach their ends.
There are 2 independent parts, one for each index of `frag`. The reference program is written for one: setup_inputs(seed, part) draws one part's arguments, and reference() takes and returns one part's arrays. A program takes and returns all parts, laid end to end along the dimension named above; each array names one. Nothing has to cross between parts.
Inputs may be any that keep to these rules, and one draw needn't show every extreme that they name: `tile_owner`: in each aligned block of 125 rows (the tiles read by one pair block) no owner is named by more than 16 rows, a bound that some block reaches. `tile_extent`: row d and row (d + 8) % 16 are equal: a pair block and its mirror share one domain. `mirror_slot`: for each pair block, its 2 entries are a permutation of 0 to 1, and the entries of the mirror block are the inverse permutation.
All inputs are finite; a program needn't handle non-finite values. No bound on the sum of `tile_mask` on one device may be relied on, other than what follows from the above.
Results may differ from the reference program's by a relative error of at most 0.002.
Values may be sent and summed in bfloat16 or wider, within the bound.
A program may use at most 128 MiB of HBM per device.

```python
import math
import jax
import jax.numpy as jnp
import numpy as np
from jax import lax

VT = 128
KDOM = 5
NAUXW = 4
PB = 2
GT_DEV = 4
DOM = 640
NEED_DEV = 125
SLOTS = 16
NPAIRS = 32
NBLK = 64
N_PAIR = 16


def draw_tile_extent(key, part):
    key = jax.random.fold_in(key, 11)
    half_rows = jax.random.randint(key, (N_PAIR // 2, KDOM), VT // 2, VT + 1, dtype=jnp.int32)
    half_rows = half_rows.at[0, 0].set(VT).at[0, 1].set(VT // 2)
    return jnp.concatenate([half_rows, half_rows], axis=0)


def draw_mirror_slot(key, part):
    key = jax.random.fold_in(key, 12)
    keys_all = jax.random.split(key, N_PAIR // 2)
    forward = jax.vmap(lambda sub_key: jax.random.permutation(sub_key, PB))(keys_all).astype(jnp.int32)
    backward = jnp.argsort(forward, axis=1, stable=True).astype(jnp.int32)
    return jnp.concatenate([forward.reshape(-1), backward.reshape(-1)])


def touch_ends(array, own_key, smallest, largest):
    extent = array.shape
    place = [jax.random.randint(jax.random.fold_in(own_key, axis), (), 0, extent[axis]) for axis in range(len(extent))]
    array = array.at[tuple(place)].set(smallest)
    longest = extent.index(max(extent))
    place[longest] = (place[longest] + 1) % extent[longest]
    return array.at[tuple(place)].set(largest)


def steps_of(key, extent, cuts, smallest, top_value):
    gain = 1.0
    for dim, shards_of in cuts:
        heights = jax.random.uniform(jax.random.fold_in(jax.random.fold_in(key, 6), dim), (shards_of,), jnp.float32, smallest / len(cuts), top_value / len(cuts))
        gain = gain * jnp.repeat(jnp.exp(heights), extent[dim] // shards_of).reshape((-1,) + (1,) * (len(extent) - 1 - dim))
    return gain


def deal_out(own_key, own, number, rows, count, top, most, lean):
    order = jax.random.permutation(own_key, count)
    packed, usual = portions_of(count, rows * top, most, lean, True), portions_of(count, rows * top, most, lean, False)
    places = jnp.arange(count)

    def named(sizes, rotation):
        used = int((sizes > 0).sum())
        fixed = max(1, used // 4)
        shifted = fixed + (places - fixed + rotation * (used - fixed)) % max(1, count - fixed)
        return jnp.zeros((count,), jnp.int32).at[order[jnp.where(places < fixed, places, shifted)]].set(jnp.asarray(sizes, jnp.int32))

    sizes = jnp.where(number % 4 == 0, named(packed, number // 4), named(usual, number - number // 4 - 1))
    mixed = jax.random.permutation(jax.random.fold_in(own, 3), count)
    donor, receiver = mixed[0:count // 2 * 2:2], mixed[1:count // 2 * 2:2]
    slack = jnp.minimum(sizes[donor] - 1, most - sizes[receiver]) // 2
    slack = jnp.where((donor == order[0]) | (receiver == order[0]) | (sizes[receiver] == 0), 0, jnp.maximum(slack, 0))
    shifted = jax.random.randint(jax.random.fold_in(own, 4), (count // 2,), 0, 1 << 20) % (slack + 1)
    sizes = sizes.at[donor].add(-shifted).at[receiver].add(shifted)
    members = jnp.searchsorted(jnp.cumsum(sizes), jnp.arange(rows * top), side="right").astype(jnp.int32)
    grid = members.reshape(top, rows).T
    grid = grid[jax.random.permutation(jax.random.fold_in(own, 1), rows)]
    rotation = jax.random.randint(jax.random.fold_in(own, 2), (rows, 1), 0, top)
    return jnp.take_along_axis(grid, (jnp.arange(top)[None, :] + rotation) % top, axis=1)


def portions_of(number_of, total, limit, slope, full):
    weights = [(1 << 20) // math.isqrt(rank ** slope) + 1 for rank in range(1, number_of + 1)]
    largest = limit if full else min(limit, max(-(-total // number_of), total * weights[0] // sum(weights)))
    least = 1 if total - largest >= number_of - 1 else 0
    counts, rest = [largest] + [least] * (number_of - 1), total - largest - least * (number_of - 1)
    while rest > 0:
        free = [i for i in range(1, number_of) if counts[i] < largest] or [i for i in range(1, number_of) if counts[i] < limit]
        whole, left = sum([weights[i] for i in free]), rest
        for i in free:
            more = min(limit - counts[i], max(1, left * weights[i] // whole), rest)
            counts[i] = counts[i] + more
            rest = rest - more
    return np.array(counts)


def centred(stream_key, dims, deviation, most, shards=(), kind=jnp.bfloat16):
    loudness = steps_of(stream_key, dims, shards, -0.22, 0.18) if shards else 1.0
    values = jax.random.normal(stream_key, dims, jnp.float32) * deviation * loudness
    return jnp.minimum(jnp.maximum(values, -most), most).astype(kind)


def setup_inputs(seed: int = 0, part: int = 0) -> dict:
    key_of = jax.random.split(jax.random.key(seed), 9)
    part_splits = jax.random.split(jax.random.fold_in(key_of[8], part), 9)
    amplitudes = centred(part_splits[0], (NPAIRS, DOM, DOM), 1.0, 6.0, ((0, 16),))
    pair_ints = centred(part_splits[1], (NPAIRS, DOM, DOM), 1.0, 6.0, ((0, 16),))
    int_tiles = centred(part_splits[2], (NBLK, VT, VT), DOM ** -0.5, 0.25, ((0, 16),))
    tile_owner_keys = jax.random.split(jax.random.fold_in(part_splits[3], 1), (N_PAIR * NEED_DEV) // NEED_DEV)
    tile_owner_turns = jax.random.permutation(jax.random.fold_in(part_splits[3], 3), (N_PAIR * NEED_DEV) // NEED_DEV)
    tile_owner = jax.vmap(lambda own, number: deal_out(jax.random.fold_in(part_splits[3], 2), own, number, NEED_DEV, N_PAIR, 1, SLOTS, 2))(tile_owner_keys, tile_owner_turns).reshape((N_PAIR * NEED_DEV, 1))
    tile_slot = touch_ends(jax.random.randint(part_splits[4], (N_PAIR * NEED_DEV,), 0, GT_DEV), jax.random.fold_in(part_splits[4], 1), 0, GT_DEV - 1).astype(jnp.int32)
    tile_extent = draw_tile_extent(jax.random.fold_in(jax.random.fold_in(key_of[8], part), 71), part)
    tile_mask = touch_ends((jax.random.randint(part_splits[6], (NPAIRS, KDOM, KDOM), 0, 4) < 3).astype(jnp.int32), jax.random.fold_in(part_splits[6], 1), 0, 1)
    mirror_slot = draw_mirror_slot(jax.random.fold_in(jax.random.fold_in(key_of[8], part), 71), part)
    return {"amplitudes": amplitudes, "pair_ints": pair_ints, "int_tiles": int_tiles, "tile_owner": tile_owner, "tile_slot": tile_slot, "tile_extent": tile_extent, "tile_mask": tile_mask, "mirror_slot": mirror_slot}


def domain_mask(tile_flags, extent_row):
    position = jnp.arange(KDOM * VT)
    live_rows = (position % VT < extent_row[position // VT]).astype(jnp.float32)
    full_flags = jnp.repeat(jnp.repeat(tile_flags.astype(jnp.float32), VT, axis=1), VT, axis=2)
    return (full_flags * live_rows[None, :, None] * live_rows[None, None, :]).astype(jnp.bfloat16)


def reference(amplitudes, pair_ints, int_tiles, tile_owner, tile_slot, tile_extent, tile_mask, mirror_slot):
    block_ids = (tile_owner[:, 0] * GT_DEV + tile_slot).astype(jnp.int32).reshape(N_PAIR, NEED_DEV)

    def one_block(inputs):
        amps, ints_block, ids_row, extent_row, flags = inputs
        dmask = domain_mask(flags, extent_row)
        masked = (amps * dmask).astype(jnp.float32)
        op_tiles = jnp.take(int_tiles, ids_row, axis=0).astype(jnp.float32)
        operators = op_tiles.reshape(1 + NAUXW, KDOM, KDOM, VT, VT).transpose(0, 1, 3, 2, 4).reshape(1 + NAUXW, DOM, DOM)
        fock_op = operators[0]
        factors = operators[1:]
        fock_term = jnp.einsum("ac,qcb->qab", fock_op, masked, precision=lax.Precision.HIGHEST) + jnp.einsum("qac,bc->qab", masked, fock_op, precision=lax.Precision.HIGHEST)
        half_ladder = jnp.einsum("pac,qcd->qpad", factors, masked, precision=lax.Precision.HIGHEST).astype(jnp.bfloat16)
        half_ladder = lax.optimization_barrier(half_ladder).astype(jnp.float32)
        ladder = jnp.einsum("qpad,pbd->qab", half_ladder, factors, precision=lax.Precision.HIGHEST)
        local_res = ints_block.astype(jnp.float32) + fock_term + ladder
        return local_res, dmask

    local_all, masks_all = lax.map(one_block, (amplitudes.reshape(N_PAIR, PB, DOM, DOM), pair_ints.reshape(N_PAIR, PB, DOM, DOM), block_ids, tile_extent, tile_mask.reshape(N_PAIR, PB, KDOM, KDOM)))
    partner = jnp.roll(local_all, N_PAIR // 2, axis=0)
    mirror = jnp.take_along_axis(partner, mirror_slot.astype(jnp.int32).reshape(N_PAIR, PB)[:, :, None, None], axis=1)
    summed = local_all + jnp.swapaxes(mirror, 2, 3)
    return (masks_all.astype(jnp.float32) * summed).reshape(NPAIRS, DOM, DOM)
```

```python
import jax
import jax.numpy as jnp
from jax import lax
from jax.sharding import PartitionSpec as P

VT = 128
KDOM = 5
NAUXW = 4
DOM = 640
NEED_DEV = 125


def passed_along(value, axis, steps):
    count = lax.axis_size(axis)
    pairs = [(source, (source + steps) % count) for source in range(count)]
    return lax.ppermute(value, axis, pairs)


def domain_mask(tile_flags, extent_row):
    position = jnp.arange(KDOM * VT)
    live_rows = (position % VT < extent_row[position // VT]).astype(jnp.float32)
    full_flags = jnp.repeat(jnp.repeat(tile_flags.astype(jnp.float32), VT, axis=1), VT, axis=2)
    return (full_flags * live_rows[None, :, None] * live_rows[None, None, :]).astype(jnp.bfloat16)


def shards(
    amplitudes, pair_ints, int_tiles, tile_owner, tile_slot, tile_extent, tile_mask, mirror_slot
):
    devices = lax.axis_size("pair")
    own_index = lax.axis_index("pair")
    ids = (tile_owner[:, 0] * int_tiles.shape[0] + tile_slot).reshape(devices, NEED_DEV)
    own_ids = lax.dynamic_index_in_dim(ids, own_index, 0, keepdims=False)
    stored = lax.all_gather(int_tiles, "pair", axis=0, tiled=True)
    op_tiles = jnp.take(stored, own_ids, axis=0)
    operators = (
        op_tiles.reshape(1 + NAUXW, KDOM, KDOM, VT, VT)
        .transpose(0, 1, 3, 2, 4)
        .reshape(1 + NAUXW, DOM, DOM)
    )
    fock_op = operators[0]
    factors = operators[1:]
    dmask = domain_mask(tile_mask, tile_extent[0])
    masked = amplitudes * dmask
    fock_term = jnp.einsum(
        "ac,qcb->qab", fock_op, masked, preferred_element_type=jnp.float32
    ) + jnp.einsum("qac,bc->qab", masked, fock_op, preferred_element_type=jnp.float32)
    local_part = pair_ints.astype(jnp.float32) + fock_term
    shift_by = devices // 2
    half_ladder = jnp.einsum(
        "pac,qcd->qpad", factors, masked, preferred_element_type=jnp.float32
    ).astype(jnp.bfloat16)
    ladder = jnp.einsum("qpad,pbd->qab", half_ladder, factors, preferred_element_type=jnp.float32)
    local_res = local_part + ladder
    partner = jnp.stack(
        [passed_along(local_res[q].astype(jnp.bfloat16), "pair", shift_by) for q in range(2)]
    )
    mirror = jnp.swapaxes(jnp.take(partner, mirror_slot, axis=0), 1, 2).astype(jnp.float32)
    return dmask.astype(jnp.float32) * (local_res + mirror)


def solution(mesh):
    in_specs = (
        P(("frag", "pair"), None, None),
        P(("frag", "pair"), None, None),
        P(("frag", "pair"), None, None),
        P("frag", None),
        P("frag"),
        P(("frag", "pair"), None),
        P(("frag", "pair"), None, None),
        P(("frag", "pair")),
    )
    out_specs = P(("frag", "pair"), None, None)
    return jax.shard_map(shards, mesh=mesh, in_specs=in_specs, out_specs=out_specs, check_vma=False)
```

```python
import functools

import jax
import jax.numpy as jnp
from jax import lax
from jax.experimental import pallas as pl
from jax.experimental.pallas import tpu as pltpu
from jax.sharding import PartitionSpec as P

VT = 128
KDOM = 5
OPS = 5
DOM = 640
NEED_DEV = 125
PB = 2
PLANE = 4
STRIPS = PB * KDOM
MESH = pl.DeviceIdType.MESH


def kernel(
    n, depth,
    ids, slots, extent, flags, amps_hbm, ints_hbm, stored, out,
    tiles, ops, amps, ints, masked, local, outgoing, incoming, final,
    own_sem, load_sem, z_send, z_recv, y_send, y_recv, c_send, c_recv,
    strip_send, strip_recv, out_sem,
):
    planes = n // PLANE
    me = lax.axis_index("pair")
    plane, place = me // PLANE, me % PLANE
    across = (place + 2) % PLANE
    twin = place // 2 * 2 + (1 - place % 2)
    y_mate, c_mate = plane * PLANE + across, plane * PLANE + twin
    mirror = lax.rem(me + n // 2, n)

    def plane_at(step):
        return lax.rem(plane + step + planes, planes)

    def block(index):
        return tiles.at[pl.ds(index * depth, depth)]

    def remote(source, target, send_sem, recv_sem, device):
        return pltpu.make_async_remote_copy(
            src_ref=source, dst_ref=target, send_sem=send_sem, recv_sem=recv_sem,
            device_id={"pair": device}, device_id_type=MESH,
        )

    loads = [
        pltpu.make_async_copy(amps_hbm, amps, load_sem.at[0]),
        pltpu.make_async_copy(ints_hbm, ints, load_sem.at[1]),
        pltpu.make_async_copy(stored, block(me), own_sem),
    ]
    for load in loads:
        load.start()

    barrier = pltpu.get_barrier_semaphore()
    for step in range(1, planes):
        pl.semaphore_signal(
            barrier, inc=1, device_id={"pair": plane_at(step) * PLANE + place},
            device_id_type=MESH,
        )
    for mate in (y_mate, c_mate):
        pl.semaphore_signal(barrier, inc=1, device_id={"pair": mate}, device_id_type=MESH)
    pl.semaphore_wait(barrier, planes + 1)

    sends = []

    def go(copy):
        copy.start()
        sends.append(copy)

    for step in range(1, planes):
        go(remote(stored, block(me), z_send.at[step], z_recv.at[step],
                  plane_at(step) * PLANE + place))
    go(remote(stored, block(me), y_send.at[0], y_recv.at[0], y_mate))
    go(remote(stored, block(me), c_send.at[0, 0], c_recv.at[0, 0], c_mate))

    def slot_sent(t):
        return jnp.where(slots[0] == t, 0, 1)

    rows_of = lax.broadcasted_iota(jnp.int32, (VT, VT), 0)
    columns_of = lax.broadcasted_iota(jnp.int32, (VT, VT), 1)

    def live(q, a, b):
        inside = (rows_of < extent[0, a]) & (columns_of < extent[0, b])
        return jnp.where(inside, flags[q, a, b].astype(jnp.float32), 0.0)

    def strip_rows(a):
        return pl.ds(pl.multiple_of(a * VT, VT), VT)

    loads[0].wait()

    def mask_strip(i, carry):
        t, a = i // KDOM, i % KDOM
        q = slot_sent(t)
        for b in range(KDOM):
            cols = slice(b * VT, (b + 1) * VT)
            value = amps[q, strip_rows(a), cols].astype(jnp.float32)
            masked[t, strip_rows(a), cols] = (value * live(q, a, b)).astype(jnp.bfloat16)
        return carry

    lax.fori_loop(0, STRIPS, mask_strip, 0)
    loads[1].wait()
    loads[2].wait()

    def forward_y(step):
        index = plane_at(-step) * PLANE + across
        remote(block(index), block(index), y_send.at[step], y_recv.at[step], y_mate).wait_recv()
        go(remote(block(index), block(index), c_send.at[1, step], c_recv.at[1, step], c_mate))

    for step in range(1, planes):
        index = plane_at(-step) * PLANE + place
        remote(block(index), block(index), z_send.at[step], z_recv.at[step], c_mate).wait_recv()
        go(remote(block(index), block(index), y_send.at[step], y_recv.at[step], y_mate))
        go(remote(block(index), block(index), c_send.at[0, step], c_recv.at[0, step], c_mate))
        forward_y(step - 1)
    forward_y(planes - 1)
    for step in range(planes):
        for half, origin in enumerate((twin, (twin + 2) % PLANE)):
            index = plane_at(-step) * PLANE + origin
            remote(block(index), block(index), c_send.at[half, step], c_recv.at[half, step],
                   c_mate).wait_recv()

    def place_tiles(i, carry):
        o, a = i // KDOM, i % KDOM
        for c in range(KDOM):
            ops[a, o, :, c * VT:(c + 1) * VT] = tiles[ids[0, i * KDOM + c]]
        return carry

    lax.fori_loop(0, OPS * KDOM, place_tiles, 0)

    def send_strip(i):
        return remote(outgoing.at[i], incoming.at[i], strip_send.at[i], strip_recv.at[i], mirror)

    def compute_strip(i, carry):
        t, a = i // KDOM, i % KDOM
        q = slot_sent(t)
        first = jnp.dot(
            ops[a].reshape(OPS * VT, DOM), masked[t], preferred_element_type=jnp.float32
        )
        total = ints[q, strip_rows(a), :].astype(jnp.float32) + first[:VT]
        for o in range(OPS):
            if o == 0:
                left = masked[t, strip_rows(a), :]
            else:
                left = first[o * VT:(o + 1) * VT].astype(jnp.bfloat16)
            total += lax.dot_general(
                left, ops[:, o].reshape(DOM, DOM), (((1,), (1,)), ((), ())),
                preferred_element_type=jnp.float32,
            )
        local[t, strip_rows(a), :] = total
        outgoing[i] = total.T.astype(jnp.bfloat16)
        send_strip(i).start()
        return carry

    lax.fori_loop(0, STRIPS, compute_strip, 0)

    def write_strip(i):
        return pltpu.make_async_copy(
            final.at[i], out.at[i // KDOM, :, strip_rows(i % KDOM)], out_sem.at[i]
        )

    def finish_strip(i, carry):
        q, b = i // KDOM, i % KDOM
        send_strip(i).wait_recv()
        mine = slots[q]
        for a in range(KDOM):
            rows = slice(a * VT, (a + 1) * VT)
            both = local[mine, rows, strip_rows(b)] + incoming[i, rows, :].astype(jnp.float32)
            final[i, rows, :] = both * live(q, a, b)
        write_strip(i).start()
        return carry

    lax.fori_loop(0, STRIPS, finish_strip, 0)

    def drain(i, carry):
        send_strip(i).wait_send()
        write_strip(i).wait()
        return carry

    lax.fori_loop(0, STRIPS, drain, 0)
    for copy in sends:
        copy.wait_send()


def shards(
    amplitudes, pair_ints, int_tiles, tile_owner, tile_slot, tile_extent, tile_mask, mirror_slot
):
    n = lax.axis_size("pair")
    depth = int_tiles.shape[0]
    planes = n // PLANE
    first = lax.axis_index("pair") * NEED_DEV
    owners = lax.dynamic_slice(tile_owner, (first, 0), (NEED_DEV, 1)).reshape(1, NEED_DEV)
    places = lax.dynamic_slice(tile_slot, (first,), (NEED_DEV,)).reshape(1, NEED_DEV)
    ids = owners * depth + places
    bf16, f32 = jnp.bfloat16, jnp.float32
    dma = pltpu.SemaphoreType.DMA
    smem, anywhere = pl.BlockSpec(memory_space=pltpu.SMEM), pl.BlockSpec(memory_space=pl.ANY)
    return pl.pallas_call(
        functools.partial(kernel, n, depth),
        out_shape=jax.ShapeDtypeStruct((PB, DOM, DOM), f32),
        in_specs=[smem] * 4 + [anywhere] * 3,
        out_specs=anywhere,
        scratch_shapes=[
            pltpu.VMEM((n * depth, VT, VT), bf16),
            pltpu.VMEM((KDOM, OPS, VT, DOM), bf16),
            pltpu.VMEM((PB, DOM, DOM), bf16),
            pltpu.VMEM((PB, DOM, DOM), bf16),
            pltpu.VMEM((PB, DOM, DOM), bf16),
            pltpu.VMEM((PB, DOM, DOM), f32),
            pltpu.VMEM((STRIPS, DOM, VT), bf16),
            pltpu.VMEM((STRIPS, DOM, VT), bf16),
            pltpu.VMEM((STRIPS, DOM, VT), f32),
            dma, dma((2,)),
            dma((planes,)), dma((planes,)), dma((planes,)), dma((planes,)),
            dma((2, planes)), dma((2, planes)),
            dma((STRIPS,)), dma((STRIPS,)), dma((STRIPS,)),
        ],
        compiler_params=pltpu.CompilerParams(
            collective_id=0, has_side_effects=True, vmem_limit_bytes=56 * 1024 * 1024
        ),
        cost_estimate=pl.CostEstimate(
            flops=20 * PB * DOM**3, bytes_accessed=7 * 1024 * 1024, transcendentals=0
        ),
    )(ids, mirror_slot, tile_extent, tile_mask, amplitudes, pair_ints, int_tiles)


def solution(mesh):
    in_specs = (
        P(("frag", "pair"), None, None),
        P(("frag", "pair"), None, None),
        P(("frag", "pair"), None, None),
        P("frag", None),
        P("frag"),
        P(("frag", "pair"), None),
        P(("frag", "pair"), None, None),
        P(("frag", "pair")),
    )
    out_specs = P(("frag", "pair"), None, None)
    return jax.shard_map(shards, mesh=mesh, in_specs=in_specs, out_specs=out_specs, check_vma=False)
```

```python
import functools

import jax
import jax.numpy as jnp
from jax import lax
from jax.experimental import pallas as pl
from jax.experimental.pallas import tpu as pltpu
from jax.sharding import PartitionSpec as P

VT = 128
KDOM = 5
OPS = 5
DOM = 640
NEED_DEV = 125
PB = 2
PLANE = 4
STRIPS = PB * KDOM
MESH = pl.DeviceIdType.MESH


def kernel(
    n, depth,
    table, slots, extent, amps_hbm, ints_hbm, stored, out,
    tiles, ops, amps, ints, masked, local, outgoing, incoming, final,
    own_sem, load_sem, z_send, z_recv, y_send, y_recv, c_send, c_recv,
    strip_send, strip_recv, out_sem,
):
    planes = n // PLANE
    me = lax.axis_index("pair")
    plane, place = me // PLANE, me % PLANE
    across = (place + 2) % PLANE
    twin = place // 2 * 2 + (1 - place % 2)
    y_mate, c_mate = plane * PLANE + across, plane * PLANE + twin
    mirror = lax.rem(me + n // 2, n)

    def plane_at(step):
        return lax.rem(plane + step + planes, planes)

    pieces = z_send.shape[2]
    size = depth // pieces

    def hop_plane(way, step):
        return plane - step if way == 0 else plane + step

    def block(index, piece):
        return tiles.at[pl.ds(index * depth + piece * size, size)]

    def remote(source, target, send_sem, recv_sem, device):
        return pltpu.make_async_remote_copy(
            src_ref=source, dst_ref=target, send_sem=send_sem, recv_sem=recv_sem,
            device_id={"pair": device}, device_id_type=MESH,
        )

    loads = [
        pltpu.make_async_copy(amps_hbm, amps, load_sem.at[0]),
        pltpu.make_async_copy(ints_hbm, ints, load_sem.at[1]),
        pltpu.make_async_copy(stored, tiles.at[pl.ds(me * depth, depth)], own_sem),
    ]
    for load in loads:
        load.start()

    barrier = pltpu.get_barrier_semaphore()
    for step in range(1, planes):
        pl.semaphore_signal(
            barrier, inc=1, device_id={"pair": plane_at(step) * PLANE + place},
            device_id_type=MESH,
        )
    for mate in (y_mate, c_mate):
        pl.semaphore_signal(barrier, inc=1, device_id={"pair": mate}, device_id_type=MESH)
    pl.semaphore_wait(barrier, planes + 1)

    def over_z(way, step, piece, origin):
        target = plane + 1 if way == 0 else plane - 1
        return remote(
            origin, block(hop_plane(way, step) * PLANE + place, piece),
            z_send.at[way, step, piece], z_recv.at[way, step, piece], target * PLANE + place,
        )

    def over_y(way, step, piece, origin):
        return remote(
            origin, block(hop_plane(way, step) * PLANE + place, piece),
            y_send.at[way, step, piece], y_recv.at[way, step, piece], y_mate,
        )

    def over_c(half, way, step, piece, origin):
        source = place if half == 0 else across
        return remote(
            origin, block(hop_plane(way, step) * PLANE + source, piece),
            c_send.at[half, way, step, piece], c_recv.at[half, way, step, piece], c_mate,
        )

    def arrived(index, piece, sem):
        held = block(index, piece)
        remote(held, held, c_send.at[0, 0, 0, piece], sem, c_mate).wait_recv()

    def can_go_on(way):
        return plane < planes - 1 if way == 0 else plane > 0

    def comes(way, step):
        return plane >= step if way == 0 else plane + step < planes

    every = [(way, step) for step in range(planes) for way in range(2) if step or not way]

    for piece in range(pieces):
        own = stored.at[pl.ds(piece * size, size)]
        for way in range(2):
            pl.when(can_go_on(way))(lambda: over_z(way, 0, piece, own).start())
        over_y(0, 0, piece, own).start()
        over_c(0, 0, 0, piece, own).start()

    def slot_sent(t):
        return jnp.where(slots[0] == t, 0, 1)

    rows_of = lax.broadcasted_iota(jnp.int32, (VT, VT), 0)
    columns_of = lax.broadcasted_iota(jnp.int32, (VT, VT), 1)

    def live(q, a, b):
        inside = (rows_of < extent[0, a]) & (columns_of < extent[0, b])
        return jnp.where(inside, table[0, NEED_DEV + q * KDOM**2 + a * KDOM + b].astype(jnp.float32), 0.0)

    def strip_rows(a):
        return pl.ds(pl.multiple_of(a * VT, VT), VT)

    loads[0].wait()

    def mask_strip(i, carry):
        t, a = i // KDOM, i % KDOM
        q = slot_sent(t)
        for b in range(KDOM):
            cols = slice(b * VT, (b + 1) * VT)
            value = amps[q, strip_rows(a), cols].astype(jnp.float32)
            masked[t, strip_rows(a), cols] = (value * live(q, a, b)).astype(jnp.bfloat16)
        return carry

    lax.fori_loop(0, STRIPS, mask_strip, 0)
    loads[1].wait()
    loads[2].wait()

    def pass_z(way, step, piece):
        index = hop_plane(way, step) * PLANE + place
        held = block(index, piece)
        arrived(index, piece, z_recv.at[way, step - 1, piece])
        pl.when(can_go_on(way))(lambda: over_z(way, step, piece, held).start())
        over_y(way, step, piece, held).start()
        over_c(0, way, step, piece, held).start()

    def pass_y(way, step, piece):
        index = hop_plane(way, step) * PLANE + across
        arrived(index, piece, y_recv.at[way, step, piece])
        over_c(1, way, step, piece, block(index, piece)).start()

    for step in range(1, planes + 1):
        for piece in range(pieces):
            for way in range(2):
                if step < planes:
                    pl.when(comes(way, step))(lambda: pass_z(way, step, piece))
        for piece in range(pieces):
            for way in range(2):
                if (way, step - 1) in every:
                    pl.when(comes(way, step - 1))(lambda: pass_y(way, step - 1, piece))

    def pass_c(way, step, piece):
        for half, origin in enumerate((twin, (twin + 2) % PLANE)):
            arrived(hop_plane(way, step) * PLANE + origin, piece, c_recv.at[half, way, step, piece])

    for way, step in every:
        for piece in range(pieces):
            pl.when(comes(way, step))(lambda: pass_c(way, step, piece))

    def place_tiles(i, carry):
        o, a = i // KDOM, i % KDOM
        for c in range(KDOM):
            ops[a, o, :, c * VT:(c + 1) * VT] = tiles[table[0, i * KDOM + c]]
        return carry

    lax.fori_loop(0, OPS * KDOM, place_tiles, 0)

    def send_strip(i):
        return remote(outgoing.at[i], incoming.at[i], strip_send.at[i], strip_recv.at[i], mirror)

    def compute_strip(i, carry):
        t, a = i // KDOM, i % KDOM
        q = slot_sent(t)
        first = jnp.dot(
            ops[a].reshape(OPS * VT, DOM), masked[t], preferred_element_type=jnp.float32
        )
        total = ints[q, strip_rows(a), :].astype(jnp.float32) + first[:VT]
        for o in range(OPS):
            if o == 0:
                left = masked[t, strip_rows(a), :]
            else:
                left = first[o * VT:(o + 1) * VT].astype(jnp.bfloat16)
            total += lax.dot_general(
                left, ops[:, o].reshape(DOM, DOM), (((1,), (1,)), ((), ())),
                preferred_element_type=jnp.float32,
            )
        local[t, strip_rows(a), :] = total
        outgoing[i] = total.T.astype(jnp.bfloat16)
        send_strip(i).start()
        return carry

    lax.fori_loop(0, STRIPS, compute_strip, 0)

    def write_strip(i):
        return pltpu.make_async_copy(
            final.at[i], out.at[i // KDOM, :, strip_rows(i % KDOM)], out_sem.at[i]
        )

    def finish_strip(i, carry):
        q, b = i // KDOM, i % KDOM
        send_strip(i).wait_recv()
        mine = slots[q]
        for a in range(KDOM):
            rows = slice(a * VT, (a + 1) * VT)
            both = local[mine, rows, strip_rows(b)] + incoming[i, rows, :].astype(jnp.float32)
            final[i, rows, :] = both * live(q, a, b)
        write_strip(i).start()
        return carry

    lax.fori_loop(0, STRIPS, finish_strip, 0)

    def drain(i, carry):
        send_strip(i).wait_send()
        write_strip(i).wait()
        return carry

    lax.fori_loop(0, STRIPS, drain, 0)
    def sent(way, step, piece):
        index = hop_plane(way, step) * PLANE + place
        over_y(way, step, piece, block(index, piece)).wait_send()
        for half in range(2):
            over_c(half, way, step, piece, block(index, piece)).wait_send()

    for way, step in every:
        for piece in range(pieces):
            pl.when(comes(way, step))(lambda: sent(way, step, piece))
    for step in range(planes - 1):
        for way in range(2):
            for piece in range(pieces):
                pl.when(comes(way, step) & can_go_on(way))(
                    lambda: over_z(way, step, piece, block(me, piece)).wait_send()
                )


def shards(
    amplitudes, pair_ints, int_tiles, tile_owner, tile_slot, tile_extent, tile_mask, mirror_slot
):
    n = lax.axis_size("pair")
    depth = int_tiles.shape[0]
    planes = n // PLANE
    pieces = 2 if depth % 2 == 0 else 1
    first = lax.axis_index("pair") * NEED_DEV
    owners = lax.dynamic_slice(tile_owner, (first, 0), (NEED_DEV, 1)).reshape(1, NEED_DEV)
    places = lax.dynamic_slice(tile_slot, (first,), (NEED_DEV,)).reshape(1, NEED_DEV)
    ids = owners * depth + places
    table = jnp.concatenate([ids, tile_mask.reshape(1, PB * KDOM**2)], axis=1)
    bf16, f32 = jnp.bfloat16, jnp.float32
    dma = pltpu.SemaphoreType.DMA
    smem, anywhere = pl.BlockSpec(memory_space=pltpu.SMEM), pl.BlockSpec(memory_space=pl.ANY)
    return pl.pallas_call(
        functools.partial(kernel, n, depth),
        out_shape=jax.ShapeDtypeStruct((PB, DOM, DOM), f32),
        in_specs=[smem] * 3 + [anywhere] * 3,
        out_specs=anywhere,
        scratch_shapes=[
            pltpu.VMEM((n * depth, VT, VT), bf16),
            pltpu.VMEM((KDOM, OPS, VT, DOM), bf16),
            pltpu.VMEM((PB, DOM, DOM), bf16),
            pltpu.VMEM((PB, DOM, DOM), bf16),
            pltpu.VMEM((PB, DOM, DOM), bf16),
            pltpu.VMEM((PB, DOM, DOM), f32),
            pltpu.VMEM((STRIPS, DOM, VT), bf16),
            pltpu.VMEM((STRIPS, DOM, VT), bf16),
            pltpu.VMEM((STRIPS, DOM, VT), f32),
            dma, dma((2,)),
            dma((2, planes, pieces)), dma((2, planes, pieces)),
            dma((2, planes, pieces)), dma((2, planes, pieces)),
            dma((2, 2, planes, pieces)), dma((2, 2, planes, pieces)),
            dma((STRIPS,)), dma((STRIPS,)), dma((STRIPS,)),
        ],
        compiler_params=pltpu.CompilerParams(
            collective_id=0, has_side_effects=True, vmem_limit_bytes=56 * 1024 * 1024
        ),
        cost_estimate=pl.CostEstimate(
            flops=20 * PB * DOM**3, bytes_accessed=7 * 1024 * 1024, transcendentals=0
        ),
    )(table, mirror_slot, tile_extent, amplitudes, pair_ints, int_tiles)


def solution(mesh):
    in_specs = (
        P(("frag", "pair"), None, None),
        P(("frag", "pair"), None, None),
        P(("frag", "pair"), None, None),
        P("frag", None),
        P("frag"),
        P(("frag", "pair"), None),
        P(("frag", "pair"), None, None),
        P(("frag", "pair")),
    )
    out_specs = P(("frag", "pair"), None, None)
    return jax.shard_map(shards, mesh=mesh, in_specs=in_specs, out_specs=out_specs, check_vma=False)
```

```python
import functools

import jax
import jax.numpy as jnp
from jax import lax
from jax.experimental import pallas as pl
from jax.experimental.pallas import tpu as pltpu
from jax.sharding import PartitionSpec as P

VT = 128
KDOM = 5
OPS = 5
DOM = 640
NEED_DEV = 125
PB = 2
PLANE = 4
STRIPS = PB * KDOM
MESH = pl.DeviceIdType.MESH


def kernel(
    n, depth,
    owners, places, slots, extent, flags, amps_hbm, ints_hbm, stored, out,
    tiles, ops, amps, ints, masked, local, outgoing, incoming, final,
    own_sem, load_sem, z_send, z_recv, y_send, y_recv, c_send, c_recv,
    strip_send, strip_recv, out_sem,
):
    planes = n // PLANE
    me = lax.axis_index("pair")
    plane, place = me // PLANE, me % PLANE
    across = (place + 2) % PLANE
    twin = place // 2 * 2 + (1 - place % 2)
    y_mate, c_mate = plane * PLANE + across, plane * PLANE + twin
    mirror = lax.rem(me + n // 2, n)

    def plane_at(step):
        return lax.rem(plane + step + planes, planes)

    pieces = z_send.shape[2]
    size = depth // pieces

    def hop_plane(way, step):
        return plane - step if way == 0 else plane + step

    def block(index, piece):
        return tiles.at[pl.ds(index * depth + piece * size, size)]

    def remote(source, target, send_sem, recv_sem, device):
        return pltpu.make_async_remote_copy(
            src_ref=source, dst_ref=target, send_sem=send_sem, recv_sem=recv_sem,
            device_id={"pair": device}, device_id_type=MESH,
        )

    loads = [
        pltpu.make_async_copy(amps_hbm, amps, load_sem.at[0]),
        pltpu.make_async_copy(ints_hbm, ints, load_sem.at[1]),
        pltpu.make_async_copy(stored, tiles.at[pl.ds(me * depth, depth)], own_sem),
    ]
    for load in loads:
        load.start()

    barrier = pltpu.get_barrier_semaphore()
    for step in range(1, planes):
        pl.semaphore_signal(
            barrier, inc=1, device_id={"pair": plane_at(step) * PLANE + place},
            device_id_type=MESH,
        )
    for mate in (y_mate, c_mate):
        pl.semaphore_signal(barrier, inc=1, device_id={"pair": mate}, device_id_type=MESH)
    pl.semaphore_wait(barrier, planes + 1)

    def over_z(way, step, piece, origin):
        target = plane + 1 if way == 0 else plane - 1
        return remote(
            origin, block(hop_plane(way, step) * PLANE + place, piece),
            z_send.at[way, step, piece], z_recv.at[way, step, piece], target * PLANE + place,
        )

    def over_y(way, step, piece, origin):
        return remote(
            origin, block(hop_plane(way, step) * PLANE + place, piece),
            y_send.at[way, step, piece], y_recv.at[way, step, piece], y_mate,
        )

    def over_c(half, way, step, piece, origin):
        source = place if half == 0 else across
        return remote(
            origin, block(hop_plane(way, step) * PLANE + source, piece),
            c_send.at[half, way, step, piece], c_recv.at[half, way, step, piece], c_mate,
        )

    def arrived(index, piece, sem):
        held = block(index, piece)
        remote(held, held, c_send.at[0, 0, 0, piece], sem, c_mate).wait_recv()

    def can_go_on(way):
        return plane < planes - 1 if way == 0 else plane > 0

    def comes(way, step):
        return plane >= step if way == 0 else plane + step < planes

    every = [(way, step) for step in range(planes) for way in range(2) if step or not way]

    for piece in range(pieces):
        own = stored.at[pl.ds(piece * size, size)]
        for way in range(2):
            pl.when(can_go_on(way))(lambda: over_z(way, 0, piece, own).start())
        over_y(0, 0, piece, own).start()
        over_c(0, 0, 0, piece, own).start()

    def slot_sent(t):
        return jnp.where(slots[0] == t, 0, 1)

    rows_of = lax.broadcasted_iota(jnp.int32, (VT, VT), 0)
    columns_of = lax.broadcasted_iota(jnp.int32, (VT, VT), 1)

    def live(q, a, b):
        inside = (rows_of < extent[0, a]) & (columns_of < extent[0, b])
        return jnp.where(inside, flags[a, q, b].astype(jnp.float32), 0.0)

    def strip_rows(a):
        return pl.ds(pl.multiple_of(a * VT, VT), VT)

    loads[0].wait()

    def mask_strip(i, carry):
        t, a = i // KDOM, i % KDOM
        q = slot_sent(t)
        for b in range(KDOM):
            cols = slice(b * VT, (b + 1) * VT)
            value = amps[q, strip_rows(a), cols].astype(jnp.float32)
            masked[t, strip_rows(a), cols] = (value * live(q, a, b)).astype(jnp.bfloat16)
        return carry

    lax.fori_loop(0, STRIPS, mask_strip, 0)
    loads[1].wait()
    loads[2].wait()

    def pass_z(way, step, piece):
        index = hop_plane(way, step) * PLANE + place
        held = block(index, piece)
        arrived(index, piece, z_recv.at[way, step - 1, piece])
        pl.when(can_go_on(way))(lambda: over_z(way, step, piece, held).start())
        over_y(way, step, piece, held).start()
        over_c(0, way, step, piece, held).start()

    def pass_y(way, step, piece):
        index = hop_plane(way, step) * PLANE + across
        arrived(index, piece, y_recv.at[way, step, piece])
        over_c(1, way, step, piece, block(index, piece)).start()

    for step in range(1, planes + 1):
        for piece in range(pieces):
            for way in range(2):
                if step < planes:
                    pl.when(comes(way, step))(lambda: pass_z(way, step, piece))
        for piece in range(pieces):
            for way in range(2):
                if (way, step - 1) in every:
                    pl.when(comes(way, step - 1))(lambda: pass_y(way, step - 1, piece))

    def pass_c(way, step, piece):
        for half, origin in enumerate((twin, (twin + 2) % PLANE)):
            arrived(hop_plane(way, step) * PLANE + origin, piece, c_recv.at[half, way, step, piece])

    for way, step in every:
        for piece in range(pieces):
            pl.when(comes(way, step))(lambda: pass_c(way, step, piece))

    def tile_at(index):
        row = me * NEED_DEV + index
        return owners[0, row] * depth + places[row]

    def place_tiles(i, carry):
        o, a = i // KDOM, i % KDOM
        for c in range(KDOM):
            ops[a, o, :, c * VT:(c + 1) * VT] = tiles[tile_at(i * KDOM + c)]
        return carry

    lax.fori_loop(0, OPS * KDOM, place_tiles, 0)

    def send_strip(i):
        return remote(outgoing.at[i], incoming.at[i], strip_send.at[i], strip_recv.at[i], mirror)

    def compute_strip(i, carry):
        t, a = i // KDOM, i % KDOM
        q = slot_sent(t)
        first = jnp.dot(
            ops[a].reshape(OPS * VT, DOM), masked[t], preferred_element_type=jnp.float32
        )
        total = ints[q, strip_rows(a), :].astype(jnp.float32) + first[:VT]
        for o in range(OPS):
            if o == 0:
                left = masked[t, strip_rows(a), :]
            else:
                left = first[o * VT:(o + 1) * VT].astype(jnp.bfloat16)
            total += lax.dot_general(
                left, ops[:, o].reshape(DOM, DOM), (((1,), (1,)), ((), ())),
                preferred_element_type=jnp.float32,
            )
        local[t, strip_rows(a), :] = total
        outgoing[i] = total.T.astype(jnp.bfloat16)
        send_strip(i).start()
        return carry

    lax.fori_loop(0, STRIPS, compute_strip, 0)

    def write_strip(i):
        return pltpu.make_async_copy(
            final.at[i], out.at[i // KDOM, :, strip_rows(i % KDOM)], out_sem.at[i]
        )

    def finish_strip(i, carry):
        q, b = i // KDOM, i % KDOM
        send_strip(i).wait_recv()
        mine = slots[q]
        for a in range(KDOM):
            rows = slice(a * VT, (a + 1) * VT)
            both = local[mine, rows, strip_rows(b)] + incoming[i, rows, :].astype(jnp.float32)
            final[i, rows, :] = both * live(q, a, b)
        write_strip(i).start()
        return carry

    lax.fori_loop(0, STRIPS, finish_strip, 0)

    def drain(i, carry):
        send_strip(i).wait_send()
        write_strip(i).wait()
        return carry

    lax.fori_loop(0, STRIPS, drain, 0)
    def sent(way, step, piece):
        index = hop_plane(way, step) * PLANE + place
        over_y(way, step, piece, block(index, piece)).wait_send()
        for half in range(2):
            over_c(half, way, step, piece, block(index, piece)).wait_send()

    for way, step in every:
        for piece in range(pieces):
            pl.when(comes(way, step))(lambda: sent(way, step, piece))
    for step in range(planes - 1):
        for way in range(2):
            for piece in range(pieces):
                pl.when(comes(way, step) & can_go_on(way))(
                    lambda: over_z(way, step, piece, block(me, piece)).wait_send()
                )


def shards(
    amplitudes, pair_ints, int_tiles, tile_owner, tile_slot, tile_extent, tile_mask, mirror_slot
):
    n = lax.axis_size("pair")
    depth = int_tiles.shape[0]
    planes = n // PLANE
    pieces = 2 if depth % 2 == 0 else 1
    bf16, f32 = jnp.bfloat16, jnp.float32
    dma = pltpu.SemaphoreType.DMA
    smem, anywhere = pl.BlockSpec(memory_space=pltpu.SMEM), pl.BlockSpec(memory_space=pl.ANY)
    return pl.pallas_call(
        functools.partial(kernel, n, depth),
        out_shape=jax.ShapeDtypeStruct((PB, DOM, DOM), f32),
        in_specs=[smem] * 5 + [anywhere] * 3,
        out_specs=anywhere,
        scratch_shapes=[
            pltpu.VMEM((n * depth, VT, VT), bf16),
            pltpu.VMEM((KDOM, OPS, VT, DOM), bf16),
            pltpu.VMEM((PB, DOM, DOM), bf16),
            pltpu.VMEM((PB, DOM, DOM), bf16),
            pltpu.VMEM((PB, DOM, DOM), bf16),
            pltpu.VMEM((PB, DOM, DOM), f32),
            pltpu.VMEM((STRIPS, DOM, VT), bf16),
            pltpu.VMEM((STRIPS, DOM, VT), bf16),
            pltpu.VMEM((STRIPS, DOM, VT), f32),
            dma, dma((2,)),
            dma((2, planes, pieces)), dma((2, planes, pieces)),
            dma((2, planes, pieces)), dma((2, planes, pieces)),
            dma((2, 2, planes, pieces)), dma((2, 2, planes, pieces)),
            dma((STRIPS,)), dma((STRIPS,)), dma((STRIPS,)),
        ],
        compiler_params=pltpu.CompilerParams(
            collective_id=0, has_side_effects=True, vmem_limit_bytes=(30 + n * depth // 32) * 1024 * 1024
        ),
        cost_estimate=pl.CostEstimate(
            flops=20 * PB * DOM**3, bytes_accessed=7 * 1024 * 1024, transcendentals=0
        ),
    )(*(
        pltpu.with_memory_space_constraint(value, pltpu.HBM)
        for value in (
            tile_owner.T, tile_slot, mirror_slot, tile_extent,
            jnp.transpose(tile_mask, (1, 0, 2)), amplitudes, pair_ints, int_tiles,
        )
    ))


def solution(mesh):
    in_specs = (
        P(("frag", "pair"), None, None),
        P(("frag", "pair"), None, None),
        P(("frag", "pair"), None, None),
        P("frag", None),
        P("frag"),
        P(("frag", "pair"), None),
        P(("frag", "pair"), None, None),
        P(("frag", "pair")),
    )
    out_specs = P(("frag", "pair"), None, None)
    return jax.shard_map(shards, mesh=mesh, in_specs=in_specs, out_specs=out_specs, check_vma=False)
```
